256 devices in a mesh: section: 16 (over z, y_hi), tensor: 8 (over x, y_lo), pool: 2 (over core).
Axes of the slice: x: 4, y: 4 (y_hi: 2, y_lo: 2; y = y_hi * 2 + y_lo), z: 8, core: 2. Of those that a mesh axis runs over, the one named last changes fastest.
Arguments:
- queries: bfloat16 [2, 16, 1024, 16384], P('pool', 'section', None, 'tensor'), may hold values from -8 to 8
- keys_values: bfloat16 [2, 16, 1024, 2048], P('pool', 'section', None, 'tensor'), may hold values from -6 to 6
- prompt_lengths: int32 [2, 4], replicated, may hold values from 1 to 256, as said below
- cache_lengths: int32 [512], replicated, may hold values from 1 to 256, as said below
- section_map: int32 [16], replicated, may hold values from 0 to 15, as said below
Outputs:
- attended: bfloat16 [2, 16, 1024, 16384], P('pool', 'section', None, 'tensor')
The draws below stay inside these ranges and needn't reach their ends.
Inputs may be any that keep to these rules, and one draw needn't show every extreme that they name: `prompt_lengths`: every micro-batch's lengths sum to 512, and one of them is 256. `cache_lengths`: A row's length is at most the length of the prompt it serves; in each micro-batch some row reads the whole of its longest prompt. `section_map`: A permutation of the layers.
All inputs are finite; a program needn't handle non-finite values.
Results may differ from the reference program's by a relative error of at most 0.0048.
Values may be sent and summed in bfloat16 or wider, within the bound.
No kernel may reach another device: no remote copies, remote signals or barrier semaphores. Data moves between devices by JAX's collectives and lax.ppermute only.
A program may use at most 128 MiB of HBM per device.

```python
import jax
import jax.numpy as jnp
from jax import lax

QUERY_HEADS = 128
KEY_VALUE_HEADS = 8
HEAD_SIZE = 128
POOL_HALF_ROWS = 1024
MB = 2
SEQS = 4
MBT = 512
R = 512
LAYER_COUNT = 16


def shared_layout(key):
    longest_len = MBT // 2
    base_key = jax.random.fold_in(key, 101)
    key_cut, key_place = jax.random.split(base_key, 2)
    cut_keys = jax.random.split(key_cut, MB)

    def one_batch(batch_key):
        cuts = jnp.sort(jax.random.permutation(batch_key, longest_len - 1)[:SEQS - 2] + 1).astype(jnp.int32)
        edges = jnp.concatenate([jnp.zeros((1,), jnp.int32), cuts, jnp.full((1,), longest_len, jnp.int32)])
        pieces = edges[1:] - edges[:-1]
        return jnp.concatenate([jnp.full((1,), longest_len, jnp.int32), pieces])
    ordered = jax.vmap(one_batch)(cut_keys)
    longest = jax.random.randint(key_place, (MB,), 0, SEQS).astype(jnp.int32)
    index = (jnp.arange(SEQS, dtype=jnp.int32)[None, :] - longest[:, None]) % SEQS
    lengths = jnp.take_along_axis(ordered, index, axis=1).astype(jnp.int32)
    return (lengths, longest)


def draw_prompt_lengths(key, part):
    lengths, longest = shared_layout(key)
    return lengths


def force_value(source, position, wanted):
    holder = jnp.argmax((source == wanted).astype(jnp.int32)).astype(jnp.int32)
    current = source[position]
    source = source.at[holder].set(current)
    return source.at[position].set(wanted)


def draw_section_map(key, part):
    key = jax.random.fold_in(key, 29)
    key_perm, key_start = jax.random.split(key)
    count = LAYER_COUNT
    source = jax.random.permutation(key_perm, count).astype(jnp.int32)
    first = jax.random.randint(key_start, (), 0, count).astype(jnp.int32)
    source = force_value(source, first, (first + count // 2) % count)
    second = (first + 1) % count
    source = force_value(source, second, first)
    sections = jnp.arange(count, dtype=jnp.int32)
    return jnp.zeros((count,), jnp.int32).at[source].set(sections)


def draw_cache_lengths(key, part):
    lengths, longest = shared_layout(key)
    key = jax.random.fold_in(key, 7)
    key_pick, key_span = jax.random.split(key)
    share = R // MB
    rows = jnp.arange(R, dtype=jnp.int32)
    batch = rows // share
    local = rows % share
    serving = jnp.take_along_axis(lengths[batch], (local % SEQS)[:, None], axis=1)[:, 0]
    partial_len = jax.random.randint(key_span, (R,), 1, serving + 1)
    pick = jax.random.randint(key_pick, (R,), 0, 4)
    chosen = jnp.where(pick == 0, serving, partial_len)
    chosen = jnp.where(local == longest[batch], serving, chosen)
    return chosen.astype(jnp.int32)


def draw_queries(key, part):
    key = jax.random.fold_in(key, 11)
    array_extent = (2, LAYER_COUNT, POOL_HALF_ROWS, QUERY_HEADS * HEAD_SIZE)
    values = jnp.clip(jax.random.normal(key, array_extent, jnp.float32), -6.0, 6.0)
    return values.astype(jnp.bfloat16)


def draw_keys_values(key, part):
    key = jax.random.fold_in(key, 13)
    array_extent = (2, LAYER_COUNT, POOL_HALF_ROWS, KEY_VALUE_HEADS * 2 * HEAD_SIZE)
    values = jnp.clip(jax.random.normal(key, array_extent, jnp.float32), -6.0, 6.0)
    return values.astype(jnp.bfloat16)


def setup_inputs(seed: int = 0) -> dict:
    arg_keys = jax.random.split(jax.random.key(seed), 6)
    return {
        "queries": draw_queries(jax.random.fold_in(arg_keys[5], 71), 0),
        "keys_values": draw_keys_values(jax.random.fold_in(arg_keys[5], 71), 0),
        "prompt_lengths": draw_prompt_lengths(jax.random.fold_in(arg_keys[5], 71), 0),
        "cache_lengths": draw_cache_lengths(jax.random.fold_in(arg_keys[5], 71), 0),
        "section_map": draw_section_map(jax.random.fold_in(arg_keys[5], 71), 0),
    }


def segment_ids(lengths, count):
    ends = jnp.cumsum(lengths.astype(jnp.int32))
    position = jnp.arange(count, dtype=jnp.int32)
    return jnp.sum((position[:, None] >= ends[None, :]).astype(jnp.int32), axis=1)


def row_starts(lengths, share):
    whole = lengths.astype(jnp.int32)
    starts = jnp.cumsum(whole) - whole
    serving = jnp.arange(share, dtype=jnp.int32) % whole.shape[0]
    chosen = (serving[:, None] == jnp.arange(whole.shape[0], dtype=jnp.int32)[None, :]).astype(jnp.int32)
    return jnp.sum(chosen * starts[None, :], axis=1)


def prompt_block(q_rows, kv_rows, segment, head_dim):
    count = q_rows.shape[0]
    groups = kv_rows.shape[1] // (2 * head_dim)
    per_group = q_rows.shape[1] // (groups * head_dim)
    q_heads = q_rows.reshape(count, groups, per_group, head_dim)
    kv_heads = kv_rows.reshape(count, groups, 2, head_dim)
    scores = jnp.einsum("qgjd,kgd->gjqk", q_heads, kv_heads[:, :, 0], preferred_element_type=jnp.float32) * (head_dim ** -0.5)
    position = jnp.arange(count, dtype=jnp.int32)
    allowed = (segment[:, None] == segment[None, :]) & (position[None, :] <= position[:, None])
    scores = jnp.where(allowed, scores, -1.0e30)
    top = jnp.max(scores, axis=-1, keepdims=True)
    weights = jnp.exp(scores - top)
    probs = (weights / jnp.sum(weights, axis=-1, keepdims=True)).astype(jnp.bfloat16)
    out = jnp.einsum("gjqk,kgd->qgjd", probs, kv_heads[:, :, 1], preferred_element_type=jnp.float32)
    return out.reshape(count, groups * per_group * head_dim).astype(jnp.bfloat16)


def prompt_attention(q_rows, kv_rows, lengths, head_dim):
    tokens = q_rows.shape[0] // lengths.shape[0]
    pieces = []
    for batch in range(lengths.shape[0]):
        segment = segment_ids(lengths[batch], tokens)
        start_row = batch * tokens
        pieces.append(prompt_block(q_rows[start_row:start_row + tokens], kv_rows[start_row:start_row + tokens], segment, head_dim))
    return jnp.concatenate(pieces, axis=0)


def decode_attention(q_rows, fresh_rows, prompt_kv, prompt_lengths, cache_lengths, batches, head_dim):
    rows = cache_lengths.shape[0]
    steps = q_rows.shape[0] // rows
    tokens = prompt_kv.shape[0] // batches
    share = rows // batches
    groups = prompt_kv.shape[1] // (2 * head_dim)
    per_group = q_rows.shape[1] // (groups * head_dim)
    fresh_all = fresh_rows.reshape(steps, rows, groups, 2, head_dim)
    scale = head_dim ** -0.5
    outs = []
    for step in range(steps):
        for batch in range(batches):
            start_row = step * rows + batch * share
            q_heads = q_rows[start_row:start_row + share].reshape(share, groups, per_group, head_dim)
            keys = prompt_kv[batch * tokens:(batch + 1) * tokens].reshape(tokens, groups, 2, head_dim)
            fresh = fresh_all[:, batch * share:(batch + 1) * share]
            reach = cache_lengths[batch * share:(batch + 1) * share].astype(jnp.int32)
            begin = row_starts(prompt_lengths[batch], share)
            old_scores = jnp.einsum("rgjd,kgd->rgjk", q_heads, keys[:, :, 0], preferred_element_type=jnp.float32) * scale
            position = jnp.arange(tokens, dtype=jnp.int32)
            inside = (position[None, :] >= begin[:, None]) & (position[None, :] < (begin + reach)[:, None])
            old_scores = jnp.where(inside[:, None, None, :], old_scores, -1.0e30)
            new_scores = jnp.einsum("rgjd,srgd->rgjs", q_heads, fresh[:, :, :, 0], preferred_element_type=jnp.float32) * scale
            taken = jnp.arange(steps, dtype=jnp.int32) <= step
            new_scores = jnp.where(taken[None, None, None, :], new_scores, -1.0e30)
            top = jnp.maximum(jnp.max(old_scores, axis=-1, keepdims=True), jnp.max(new_scores, axis=-1, keepdims=True))
            old_weights = jnp.exp(old_scores - top)
            new_weights = jnp.exp(new_scores - top)
            total = jnp.sum(old_weights, axis=-1, keepdims=True) + jnp.sum(new_weights, axis=-1, keepdims=True)
            old_probs = (old_weights / total).astype(jnp.bfloat16)
            new_probs = (new_weights / total).astype(jnp.bfloat16)
            out = jnp.einsum("rgjk,kgd->rgjd", old_probs, keys[:, :, 1], preferred_element_type=jnp.float32)
            out = out + jnp.einsum("rgjs,srgd->rgjd", new_probs, fresh[:, :, :, 1], preferred_element_type=jnp.float32)
            outs.append(out.reshape(share, groups * per_group * head_dim).astype(jnp.bfloat16))
    return jnp.concatenate(outs, axis=0)


def reference(queries, keys_values, prompt_lengths, cache_lengths, section_map):
    layer_ids = jnp.arange(LAYER_COUNT, dtype=jnp.int32)

    def prefill_layer(layer):
        return prompt_attention(queries[0, layer], keys_values[0, layer], prompt_lengths, HEAD_SIZE)

    def decode_slot(slot):
        source = jnp.sum(layer_ids * (section_map == slot).astype(jnp.int32))
        return decode_attention(queries[1, slot], keys_values[1, slot], keys_values[0, source], prompt_lengths, cache_lengths, MB, HEAD_SIZE)

    first = lax.map(prefill_layer, layer_ids)
    second = lax.map(decode_slot, layer_ids)
    return jnp.stack([first, second], axis=0)
```

```python
import functools
import math

import jax
import jax.numpy as jnp
from jax import lax
from jax.experimental import pallas as pl
from jax.experimental.pallas import tpu as pltpu
from jax.sharding import PartitionSpec as P

HEAD_SIZE = 128
RATE = HEAD_SIZE ** (-0.5) * math.log2(math.e)
NEVER = -1e30
VMEM_LIMIT = 48 * 1024 * 1024
F32 = jnp.float32
BF16 = jnp.bfloat16


def nt_dot(a, b):
    return lax.dot_general(a, b, (((1,), (1,)), ((), ())), preferred_element_type=F32)


def iota(shape, dim):
    return lax.broadcasted_iota(jnp.int32, shape, dim)


def prefill(plen, q_ref, kv_ref, buf_ref):
    ones = jnp.ones((384, HEAD_SIZE), BF16)
    for m in range(2):
        for i in range(4):
            first = max(0, i - 2) * 128
            width = (i + 1) * 128 - first
            row0 = m * 512 + i * 128
            keys = kv_ref[m * 512 + first : m * 512 + first + width, 0:HEAD_SIZE]
            values = kv_ref[m * 512 + first : m * 512 + first + width, HEAD_SIZE:]
            values = jnp.concatenate([values, ones[:width]], axis=1)
            token = iota((128, width), 0) + i * 128
            key = iota((128, width), 1) + first
            begin = jnp.zeros((128, width), jnp.int32)
            end = jnp.int32(0)
            for c in range(4):
                end = end + plen[m, c]
                begin = jnp.where(token >= end, end, begin)
            bias = jnp.where((key >= begin) & (key <= token), 0.0, NEVER).astype(F32)

            def quad(hq, carry):
                base = pl.multiple_of(hq * 512, 512)
                q4 = q_ref[row0 : row0 + 128, pl.ds(base, 512)]
                q4 = jnp.concatenate([q4[:, h * 128 : (h + 1) * 128] for h in range(4)], axis=0)
                s = nt_dot(q4, keys)
                s = (s.reshape(4, 128, width) + bias[None]).reshape(512, width)
                top = jnp.max(s, axis=1, keepdims=True)
                p = jnp.exp2((s - top) * RATE).astype(BF16)
                o = jnp.dot(p, values, preferred_element_type=F32)
                o = (o[:, :128] / o[:, 128:]).astype(BF16)
                for h in range(4):
                    buf_ref[row0 : row0 + 128, pl.ds(base + h * 128, 128)] = o[
                        h * 128 : (h + 1) * 128
                    ]
                return carry

            lax.fori_loop(0, 4, quad, 0)


def prepare(q_ref, kv_ref, cache_ref, buf_ref, sn_ref, vft_ref, len_ref):
    new = iota((512, 512), 0)
    place = ((new >> 6) & 1) * 256 + (new & 63) * 4 + (new >> 7)
    perm = (iota((512, 512), 1) == place).astype(F32).astype(BF16)
    new = iota((512, 256), 0)
    local = (iota((512, 256), 1) == (new & 63) * 4 + (new >> 7)).astype(F32).astype(BF16)
    eye = (iota((128, 128), 0) == iota((128, 128), 1)).astype(F32).astype(BF16)
    ones = jnp.ones((8, 256), BF16)
    lane = iota((8, 512), 1)
    row = iota((8, 512), 0)
    for m in range(2):
        lens = cache_ref[0:1, m * 256 : (m + 1) * 256].astype(F32).astype(BF16)
        lens = jnp.broadcast_to(lens, (8, 256))
        len_ref[m * 8 : (m + 1) * 8, :] = nt_dot(lens, local)
        kvm = jnp.concatenate(
            [kv_ref[m * 256 : (m + 1) * 256, :], kv_ref[512 + m * 256 : 512 + (m + 1) * 256, :]],
            axis=0,
        )
        fresh = jnp.dot(perm, kvm, preferred_element_type=F32)
        for c in range(4):
            vf = fresh[c * 128 : (c + 1) * 128, HEAD_SIZE:].astype(BF16)
            at = (m * 4 + c) * 128
            vft_ref[at : at + 128, :] = nt_dot(eye, vf).astype(BF16)

        def quad(hq, carry):
            base = pl.multiple_of(hq * 512, 512)
            qm = jnp.concatenate(
                [
                    q_ref[m * 256 : (m + 1) * 256, pl.ds(base, 512)],
                    q_ref[512 + m * 256 : 512 + (m + 1) * 256, pl.ds(base, 512)],
                ],
                axis=0,
            )
            qp = jnp.dot(perm, qm, preferred_element_type=F32)
            buf_ref[m * 512 : (m + 1) * 512, pl.ds(base, 512)] = qp.astype(BF16)
            for c in range(4):
                got = []
                for step in range(2):
                    at = c * 128 + step * 64
                    kf = fresh[at : at + 64, :HEAD_SIZE]
                    kf = jnp.concatenate([kf, kf], axis=0)
                    parts = []
                    for h in range(4):
                        part = qp[c * 128 : (c + 1) * 128, h * 128 : (h + 1) * 128] * kf
                        high = part.astype(BF16)
                        low = (part - high.astype(F32)).astype(BF16)
                        parts.append(jnp.concatenate([high, low], axis=1))
                    got.append(nt_dot(ones, jnp.concatenate(parts, axis=0)))
                later = jnp.where(((lane >> 6) & 1) == 1, got[1], NEVER)
                at = (m * 4 + c) * 8
                sn_ref[at : at + 8, pl.ds(base, 512)] = jnp.where(row < 4, got[0], later)
            return carry

        lax.fori_loop(0, 4, quad, 0)


def first_kernel(pool, plen, q_ref, kv_ref, cache_ref, buf_ref, sn_ref, vft_ref, len_ref):
    @pl.when(pool[0] == 0)
    def _():
        prefill(plen, q_ref, kv_ref, buf_ref)

    @pl.when(pool[0] != 0)
    def _():
        prepare(q_ref, kv_ref, cache_ref, buf_ref, sn_ref, vft_ref, len_ref)


def first_part(pool, plen, queries, kv, cache):
    whole = pl.BlockSpec(memory_space=pltpu.VMEM)
    scalar = pl.BlockSpec(memory_space=pltpu.SMEM)
    return pl.pallas_call(
        first_kernel,
        out_shape=(
            jax.ShapeDtypeStruct((1024, 2048), BF16),
            jax.ShapeDtypeStruct((64, 2048), F32),
            jax.ShapeDtypeStruct((1024, 128), BF16),
            jax.ShapeDtypeStruct((16, 512), F32),
        ),
        in_specs=[scalar, scalar, whole, whole, whole],
        out_specs=(whole,) * 4,
        compiler_params=pltpu.CompilerParams(vmem_limit_bytes=VMEM_LIMIT),
    )(pool, plen, queries, kv, cache)


def group_rows(n, g, begin, kvf, qv, sn_ref, vft_ref, len_ref, ot):
    m, c = g // 4, g % 4
    size = n * 128
    eye = (iota((128, 128), 0) == iota((128, 128), 1)).astype(F32).astype(BF16)
    reach = size + 16
    window = kvf[pl.ds(pl.multiple_of((begin >> 3) * 8, 8), reach), :]
    window = pltpu.roll(window, reach - (begin & 7), 0)[:size].astype(BF16)
    keys = window[:, 0:HEAD_SIZE]
    values = window[:, HEAD_SIZE:]
    g128 = pl.multiple_of(g * 128, 128)
    values = jnp.concatenate(
        [nt_dot(eye, values).astype(BF16), vft_ref[pl.ds(g128, 128), :]], axis=1
    )
    lens = len_ref[pl.ds(pl.multiple_of(m * 8, 8), 1), pl.ds(pl.multiple_of(c * 128, 128), 128)]
    bias = jnp.where(iota((size, 128), 0).astype(F32) < lens, 0.0, NEVER).astype(F32)
    bias = jnp.concatenate([bias] * 4, axis=1)
    own = iota((64, 512), 0) == (iota((64, 512), 1) & 63)

    def quad(hq, carry):
        base = pl.multiple_of(hq * 512, 512)
        q4 = qv[pl.ds(g128, 128), pl.ds(base, 512)]
        q4 = jnp.concatenate([q4[:, h * 128 : (h + 1) * 128] for h in range(4)], axis=0)
        s = nt_dot(keys, q4) + bias
        fresh = sn_ref[pl.ds(pl.multiple_of(g * 8, 8), 8), pl.ds(base, 512)]
        s0, s1 = fresh[0:1], fresh[4:5]
        top = jnp.maximum(jnp.max(s, axis=0, keepdims=True), jnp.maximum(s0, s1))
        p = jnp.exp2((s - top) * RATE)
        p0 = jnp.exp2((s0 - top) * RATE)
        p1 = jnp.exp2((s1 - top) * RATE)
        total = jnp.sum(p, axis=0, keepdims=True) + p0 + p1
        p = jnp.concatenate(
            [
                p.astype(BF16),
                jnp.where(own, p0, 0.0).astype(BF16),
                jnp.where(own, p1, 0.0).astype(BF16),
            ],
            axis=0,
        )
        o = jnp.dot(values, p, preferred_element_type=F32)
        ot[c, :, pl.ds(base, 512)] = o * (1.0 / total)
        return carry

    lax.fori_loop(0, 4, quad, 0)


def second_kernel(
    pool, plen, kv_ref, sn_ref, vft_ref, len_ref, buf_in, buf_out, qv, ov, kvf, ot, in_sem, out_sem
):
    del buf_in

    @pl.when(pool[0] != 0)
    def _():
        loads = [
            pltpu.make_async_copy(
                buf_out.at[pl.ds(m * 512, 512)], qv.at[pl.ds(m * 512, 512)], in_sem.at[m]
            )
            for m in range(2)
        ]
        for load in loads:
            load.start()
        kvf[512:784, :] = jnp.zeros((272, 256), F32)
        new = iota((256, 256), 1)
        back = (iota((256, 256), 0) == (new & 63) * 4 + (new >> 6)).astype(F32).astype(BF16)
        left = iota((128, 128), 1) < 64
        stores = []
        for m in range(2):
            kvf[0:512, :] = kv_ref[m * 512 : (m + 1) * 512, :].astype(F32)
            loads[m].wait()

            def one(c, begin):
                length = plen[m, c]

                @pl.when(length <= 128)
                def _():
                    group_rows(1, m * 4 + c, begin, kvf, qv, sn_ref, vft_ref, len_ref, ot)

                @pl.when(length > 128)
                def _():
                    group_rows(2, m * 4 + c, begin, kvf, qv, sn_ref, vft_ref, len_ref, ot)

                return begin + length

            lax.fori_loop(0, 4, one, jnp.int32(0))

            def pair(hp, carry):
                base = pl.multiple_of(hp * 256, 256)
                sides = [[], []]
                for h in range(2):
                    t = [ot[c, :, pl.ds(base + h * 128, 128)] for c in range(4)]
                    r = [pltpu.roll(x, 64, 1) for x in t]
                    sides[0].append(
                        jnp.concatenate(
                            [jnp.where(left, t[0], r[1]), jnp.where(left, t[2], r[3])], axis=1
                        )
                    )
                    sides[1].append(
                        jnp.concatenate(
                            [jnp.where(left, r[0], t[1]), jnp.where(left, r[2], t[3])], axis=1
                        )
                    )
                for j in range(2):
                    w = jnp.concatenate(sides[j], axis=0).astype(BF16)
                    at = j * 512 + m * 256
                    ov[at : at + 256, pl.ds(base, 256)] = nt_dot(back, w).astype(BF16)
                return carry

            lax.fori_loop(0, 8, pair, 0)
            if m == 0:
                loads[1].wait()
                loads[1] = None
            for j in range(2):
                at = j * 512 + m * 256
                store = pltpu.make_async_copy(
                    ov.at[pl.ds(at, 256)], buf_out.at[pl.ds(at, 256)], out_sem.at[m * 2 + j]
                )
                store.start()
                stores.append(store)
            if m == 0:
                loads[1] = _Done()
        for store in stores:
            store.wait()


class _Done:
    def wait(self):
        pass


def second_part(pool, plen, kv, sn, vft, lens, buf):
    whole = pl.BlockSpec(memory_space=pltpu.VMEM)
    scalar = pl.BlockSpec(memory_space=pltpu.SMEM)
    anywhere = pl.BlockSpec(memory_space=pltpu.HBM)
    return pl.pallas_call(
        second_kernel,
        out_shape=jax.ShapeDtypeStruct((1024, 2048), BF16),
        in_specs=[scalar, scalar, whole, whole, whole, whole, anywhere],
        out_specs=anywhere,
        scratch_shapes=[
            pltpu.VMEM((1024, 2048), BF16),
            pltpu.VMEM((1024, 2048), BF16),
            pltpu.VMEM((784, 256), F32),
            pltpu.VMEM((4, 128, 2048), F32),
            pltpu.SemaphoreType.DMA((2,)),
            pltpu.SemaphoreType.DMA((4,)),
        ],
        input_output_aliases={6: 0},
        compiler_params=pltpu.CompilerParams(vmem_limit_bytes=VMEM_LIMIT),
    )(pool, plen, kv, sn, vft, lens, buf)


def body(queries, keys_values, prompt_lengths, cache_lengths, section_map):
    section = lax.axis_index("section")
    pool = lax.axis_index("pool")
    count = lax.axis_size("section")
    layers = jnp.arange(count, dtype=jnp.int32)
    source = jnp.sum(layers * (section_map == section).astype(jnp.int32))
    target = jnp.sum(section_map * (layers == section).astype(jnp.int32))
    apart = jnp.where(pool == 0, target - section, section - source) % count
    who = pool.reshape(1).astype(jnp.int32)
    q = queries[0, 0]
    kv = keys_values[0, 0]
    cache = cache_lengths[None, :]

    def route(by):
        pairs = [(2 * s, 2 * ((s + by) % count) + 1) for s in range(count)]

        def run(who, plen, q, kv, cache):
            arrived = lax.ppermute(kv, ("section", "pool"), pairs)
            return (arrived, *first_part(who, plen, q, kv, cache))

        return run

    arrived, buf, sn, vft, lens = lax.switch(
        apart, [route(by) for by in range(count)], who, prompt_lengths, q, kv, cache
    )
    out = second_part(who, prompt_lengths, arrived, sn, vft, lens, buf)
    return out[None, None]


def solution(mesh):
    return jax.shard_map(
        body,
        mesh=mesh,
        in_specs=(
            P("pool", "section", None, "tensor"),
            P("pool", "section", None, "tensor"),
            P(),
            P(),
            P(),
        ),
        out_specs=P("pool", "section", None, "tensor"),
        check_vma=False,
    )
```

```python
import math

import jax
import jax.numpy as jnp
from jax import lax
from jax.experimental import pallas as pl
from jax.experimental.pallas import tpu as pltpu
from jax.sharding import PartitionSpec as P

HEAD_SIZE = 128
RATE = HEAD_SIZE ** (-0.5) * math.log2(math.e)
NEVER = -1e30
VMEM_LIMIT = 56 * 1024 * 1024
F32 = jnp.float32
BF16 = jnp.bfloat16


def nt_dot(a, b):
    return lax.dot_general(a, b, (((1,), (1,)), ((), ())), preferred_element_type=F32)


def dot(a, b):
    return jnp.dot(a, b, preferred_element_type=F32)


def iota(shape, dim):
    return lax.broadcasted_iota(jnp.int32, shape, dim)


def prefill(plen, q_hbm, kv_ref, out_hbm, qv, ov, bias_ref, in_sem, out_sem):
    def columns(n):
        return pl.ds(pl.multiple_of(n * 512, 512), 512)

    def load(n):
        return pltpu.make_async_copy(q_hbm.at[:, columns(n)], qv.at[n], in_sem.at[n])

    def store(n):
        return pltpu.make_async_copy(ov.at[n], out_hbm.at[:, columns(n)], out_sem.at[n])

    for n in range(4):
        load(n).start()
    steps = [(m, i) for m in range(2) for i in range(4)]
    first = [max(0, i - 2) * 128 for i in range(4)]
    width = [(i + 1) * 128 - first[i] for i in range(4)]
    for m, i in steps:
        token = iota((128, width[i]), 0) + i * 128
        key = iota((128, width[i]), 1) + first[i]
        begin = jnp.zeros((128, width[i]), jnp.int32)
        end = jnp.int32(0)
        for c in range(4):
            end = end + plen[m, c]
            begin = jnp.where(token >= end, end, begin)
        allowed = (key >= begin) & (key <= token)
        bias_ref[m, i, :, 0 : width[i]] = jnp.where(allowed, 0.0, NEVER).astype(F32)

    def score(n, m, i):
        row, k0 = m * 512 + i * 128, m * 512 + first[i]
        q4 = qv[n, row : row + 128, :]
        q4 = jnp.concatenate([q4[:, h * 128 : (h + 1) * 128] for h in range(4)], axis=0)
        return nt_dot(q4, kv_ref[k0 : k0 + width[i], 0:128])

    def finish(n, m, i, s):
        row, k0 = m * 512 + i * 128, m * 512 + first[i]
        bias = bias_ref[m, i, :, 0 : width[i]]
        s = (s.reshape(4, 128, width[i]) + bias[None]).reshape(512, width[i])
        top = jnp.max(s, axis=1, keepdims=True) * RATE
        p = jnp.exp2(s * RATE - top).astype(BF16)
        total = jnp.sum(p.astype(F32), axis=1, keepdims=True)
        o = dot(p, kv_ref[k0 : k0 + width[i], 128:256])
        o = (o * (1.0 / total)).astype(BF16)
        for h in range(4):
            ov[n, row : row + 128, h * 128 : (h + 1) * 128] = o[h * 128 : (h + 1) * 128]

    def chunk(n, carry):
        load(n).wait()
        ahead = score(n, *steps[0])
        for at, step in enumerate(steps):
            s = ahead
            if at + 1 < len(steps):
                ahead = score(n, *steps[at + 1])
            finish(n, *step, s)
        store(n).start()
        return carry

    lax.fori_loop(0, 4, chunk, 0)
    for n in range(4):
        store(n).wait()


def decode(
    plen, q_hbm, own_ref, kv_ref, cache_ref, out_hbm, qv, ov, qf, of, ownf, kvf, lens, in_sem, out_sem
):
    def load(m, j):
        at = j * 512 + m * 256
        return pltpu.make_async_copy(q_hbm.at[pl.ds(at, 256)], qv.at[m, j], in_sem.at[m * 2 + j])

    def store(m, j):
        at = j * 512 + m * 256
        return pltpu.make_async_copy(ov.at[m, j], out_hbm.at[pl.ds(at, 256)], out_sem.at[m * 2 + j])

    for m in range(2):
        for j in range(2):
            load(m, j).start()
    kvf[512:784, :] = jnp.zeros((272, 256), F32)
    lane, row = iota((16, 256), 1), iota((16, 256), 0)
    fits = ((row & 7) == (lane & 7)) & ((row >> 3) <= ((lane >> 3) & 1))
    own_bias = jnp.where(fits, 0.0, NEVER).astype(F32)
    band = iota((128, 256), 0) >> 4
    same = ((iota((256, 256), 0) >> 2) & 7) == (iota((256, 256), 1) & 7)
    same = same.astype(F32).astype(BF16)
    spot, block = iota((64, 256), 1), iota((64, 256), 0) >> 3
    for m in range(2):
        reach = cache_ref[0:1, m * 256 : (m + 1) * 256].astype(F32)
        reach = jnp.broadcast_to(reach, (64, 256))
        for c in range(4):
            mine = ((spot >> 5) == block) & ((spot & 3) == c)
            found = dot(jnp.where(mine, reach, 0.0).astype(BF16), same)
            at = (m * 4 + c) * 8
            lens[at : at + 8] = found.reshape(8, 8, 256)

    for m in range(2):
        kvf[0:512, :] = kv_ref[m * 512 : (m + 1) * 512, :].astype(F32)
        for s in range(2):
            at = s * 512 + m * 256
            for x in range(2):
                part = own_ref[at : at + 256, x * 128 : (x + 1) * 128].astype(F32)
                ownf[s * 8 : (s + 1) * 8, x] = part.reshape(8, 32, 128)
            load(m, s).wait()

        def widen(b, carry, m=m):
            for j in range(2):
                wide = qv[m, j, pl.ds(pl.multiple_of(b * 32, 32), 32), :].astype(F32)
                for h in range(16):
                    qf[j * 8 + b, h] = wide[:, h * 128 : (h + 1) * 128]
            return carry

        lax.fori_loop(0, 8, widen, 0)
        begin = jnp.int32(0)
        for c in range(4):
            length = plen[m, c]

            def group(tiles, m=m, c=c, begin=begin):
                size = tiles * 128
                reach = size + 16
                window = kvf[pl.ds(pl.multiple_of((begin >> 3) * 8, 8), reach), :]
                window = pltpu.roll(window, reach - (begin & 7), 0)[:size]
                keys = window[:, 0:128].astype(BF16)
                own = [
                    ownf[s * 8 + b, 1, pl.ds(c, 8, stride=4), :] for b in range(8) for s in range(2)
                ]
                own = jnp.concatenate(own, axis=0)
                values = jnp.concatenate([window[:, 128:256].T, own.T], axis=1).astype(BF16)
                position = iota((size, 256), 0).astype(F32)

                def score(b):
                    q = [
                        qf[j * 8 + b, h, pl.ds(c, 8, stride=4), :]
                        for h in range(16)
                        for j in range(2)
                    ]
                    q = jnp.concatenate(q, axis=0).astype(BF16)
                    own = [ownf[s * 8 + b, 0, pl.ds(c, 8, stride=4), :] for s in range(2)]
                    own = jnp.concatenate(own, axis=0).astype(BF16)
                    return nt_dot(jnp.concatenate([keys, own], axis=0), q)

                def finish(b, s):
                    inside = position < lens[(m * 4 + c) * 8 + b, 0:1, :]
                    old = jnp.where(inside, s[:size], NEVER)
                    new = s[size:] + own_bias
                    top = jnp.maximum(
                        jnp.max(old, axis=0, keepdims=True), jnp.max(new, axis=0, keepdims=True)
                    )
                    top = top * RATE
                    old = jnp.exp2(old * RATE - top)
                    new = jnp.exp2(new * RATE - top)
                    total = jnp.sum(old, axis=0, keepdims=True) + jnp.sum(new, axis=0, keepdims=True)
                    new = jnp.where(band == b, jnp.concatenate([new] * 8, axis=0), 0.0)
                    p = jnp.concatenate([old.astype(BF16), new.astype(BF16)], axis=0)
                    o = (dot(values, p) * (1.0 / total)).T
                    for h in range(16):
                        for j in range(2):
                            at = (h * 2 + j) * 8
                            of[j * 8 + b, h, pl.ds(c, 8, stride=4), :] = o[at : at + 8]

                scores = [score(b) for b in range(8)]
                for b in range(8):
                    finish(b, scores[b])

            pl.when(length <= 128)(lambda: group(1))
            pl.when(length > 128)(lambda: group(2))
            begin = begin + length

        def narrow(b, carry, m=m):
            for j in range(2):
                for h in range(16):
                    ov[m, j, pl.ds(pl.multiple_of(b * 32, 32), 32), h * 128 : (h + 1) * 128] = of[
                        j * 8 + b, h
                    ].astype(BF16)
            return carry

        lax.fori_loop(0, 8, narrow, 0)
        for j in range(2):
            store(m, j).start()
    for m in range(2):
        for j in range(2):
            store(m, j).wait()


def kernel(pool, plen, q_hbm, own_ref, kv_ref, cache_ref, out_hbm, *scratch):
    pq, po, bias, dq, do, qf, of, ownf, kvf, lens, in_sem, out_sem = scratch

    @pl.when(pool[0] == 0)
    def _():
        prefill(plen, q_hbm, own_ref, out_hbm, pq, po, bias, in_sem, out_sem)

    @pl.when(pool[0] != 0)
    def _():
        decode(
            plen, q_hbm, own_ref, kv_ref, cache_ref, out_hbm, dq, do, qf, of, ownf, kvf, lens,
            in_sem, out_sem,
        )


def attend(pool, plen, q, own, kv, cache):
    vmem = pl.BlockSpec(memory_space=pltpu.VMEM)
    smem = pl.BlockSpec(memory_space=pltpu.SMEM)
    hbm = pl.BlockSpec(memory_space=pltpu.HBM)
    return pl.pallas_call(
        kernel,
        out_shape=jax.ShapeDtypeStruct((1024, 2048), BF16),
        in_specs=[smem, smem, hbm, vmem, vmem, vmem],
        out_specs=hbm,
        scratch_shapes=[
            pltpu.VMEM((4, 1024, 512), BF16),
            pltpu.VMEM((4, 1024, 512), BF16),
            pltpu.VMEM((2, 4, 128, 384), F32),
            pltpu.VMEM((2, 2, 256, 2048), BF16),
            pltpu.VMEM((2, 2, 256, 2048), BF16),
            pltpu.VMEM((16, 16, 32, 128), F32),
            pltpu.VMEM((16, 16, 32, 128), F32),
            pltpu.VMEM((16, 2, 32, 128), F32),
            pltpu.VMEM((784, 256), F32),
            pltpu.VMEM((64, 8, 256), F32),
            pltpu.SemaphoreType.DMA((4,)),
            pltpu.SemaphoreType.DMA((4,)),
        ],
        compiler_params=pltpu.CompilerParams(vmem_limit_bytes=VMEM_LIMIT),
    )(pool, plen, q, own, kv, cache)


def body(queries, keys_values, prompt_lengths, cache_lengths, section_map):
    section = lax.axis_index("section")
    pool = lax.axis_index("pool")
    count = lax.axis_size("section")
    layers = jnp.arange(count, dtype=jnp.int32)
    source = jnp.sum(layers * (section_map == section).astype(jnp.int32))
    target = jnp.sum(section_map * (layers == section).astype(jnp.int32))
    apart = jnp.where(pool == 0, target - section, section - source) % count
    kv = keys_values[0, 0]

    def route(by):
        pairs = [(2 * s, 2 * ((s + by) % count) + 1) for s in range(count)]
        return lambda kv: lax.ppermute(kv, ("section", "pool"), pairs)

    arrived = lax.switch(apart, [route(by) for by in range(count)], kv)
    who = pool.reshape(1).astype(jnp.int32)
    out = attend(who, prompt_lengths, queries[0, 0], kv, arrived, cache_lengths[None, :])
    return out[None, None]


def solution(mesh):
    return jax.shard_map(
        body,
        mesh=mesh,
        in_specs=(
            P("pool", "section", None, "tensor"),
            P("pool", "section", None, "tensor"),
            P(),
            P(),
            P(),
        ),
        out_specs=P("pool", "section", None, "tensor"),
        check_vma=False,
    )
```

```python
import math

import jax
import jax.numpy as jnp
from jax import lax
from jax.experimental import pallas as pl
from jax.experimental.pallas import tpu as pltpu
from jax.sharding import PartitionSpec as P

HEAD_SIZE = 128
RATE = HEAD_SIZE ** (-0.5) * math.log2(math.e)
NEVER = -1e30
F32 = jnp.float32
BF16 = jnp.bfloat16


def nt_dot(a, b):
    return lax.dot_general(a, b, (((1,), (1,)), ((), ())), preferred_element_type=F32)


def dot(a, b):
    return jnp.dot(a, b, preferred_element_type=F32)


def iota(shape, dim):
    return lax.broadcasted_iota(jnp.int32, shape, dim)


def spread(wide, part, to):
    for j in range(2):
        wide[j] = part(j).astype(F32)
    for c in range(4):
        pair = [wide[j, pl.ds(c, 8, stride=4), :] for j in range(2)]
        to(c, jnp.concatenate(pair, axis=0).astype(BF16))


def regroup_kernel(q_hbm, qx, qv, wide, in_sem):
    @pl.when(lax.axis_index("pool") != 0)
    def _():
        def load(n):
            part = pl.ds(pl.multiple_of(n * 256, 256), 256)
            return pltpu.make_async_copy(q_hbm.at[part], qv.at[n], in_sem.at[n])

        lax.fori_loop(0, 4, lambda n, carry: (load(n).start(), carry)[1], 0)
        lax.fori_loop(0, 4, lambda n, carry: (load(n).wait(), carry)[1], 0)

        def piece(n, carry):
            m, b, h = n >> 7, (n >> 4) & 7, n & 15

            def part(j):
                lanes = pl.ds(pl.multiple_of(h * 128, 128), 128)
                return qv[j * 2 + m, pl.ds(pl.multiple_of(b * 32, 32), 32), lanes]

            def to(c, block):
                qx[(m * 4 + c) * 8 + b, pl.ds(pl.multiple_of(h * 16, 16), 16), :] = block

            spread(wide, part, to)
            return carry

        lax.fori_loop(0, 256, piece, 0)


def regroup(q):
    hbm = pl.BlockSpec(memory_space=pltpu.HBM)
    return pl.pallas_call(
        regroup_kernel,
        out_shape=jax.ShapeDtypeStruct((64, 256, 128), BF16),
        in_specs=[hbm],
        out_specs=pl.BlockSpec(memory_space=pltpu.VMEM),
        scratch_shapes=[
            pltpu.VMEM((4, 256, 2048), BF16),
            pltpu.VMEM((2, 32, 128), F32),
            pltpu.SemaphoreType.DMA((4,)),
        ],
        compiler_params=pltpu.CompilerParams(vmem_limit_bytes=14 * 1024 * 1024),
    )(q)


def prefill(plen, q_hbm, own_hbm, out_hbm, qv, kv_ref, ov, bias_ref, kv_sem, in_sem, out_sem):
    def columns(n):
        return pl.ds(pl.multiple_of(n * 512, 512), 512)

    def load(n):
        return pltpu.make_async_copy(q_hbm.at[:, columns(n)], qv.at[n], in_sem.at[n])

    def store(n):
        return pltpu.make_async_copy(ov.at[n], out_hbm.at[:, columns(n)], out_sem.at[n])

    own_load = pltpu.make_async_copy(own_hbm, kv_ref, kv_sem.at[0])
    own_load.start()
    for n in range(4):
        load(n).start()
    steps = [(m, i) for m in range(2) for i in range(4)]
    first = [max(0, i - 2) * 128 for i in range(4)]
    width = [(i + 1) * 128 - first[i] for i in range(4)]
    for m, i in steps:
        token = iota((128, width[i]), 0) + i * 128
        key = iota((128, width[i]), 1) + first[i]
        begin = jnp.zeros((128, width[i]), jnp.int32)
        end = jnp.int32(0)
        for c in range(4):
            end = end + plen[m, c]
            begin = jnp.where(token >= end, end, begin)
        allowed = (key >= begin) & (key <= token)
        bias_ref[m, i, :, 0 : width[i]] = jnp.where(allowed, 0.0, NEVER).astype(F32)

    def score(n, m, i):
        row, k0 = m * 512 + i * 128, m * 512 + first[i]
        q4 = qv[n, row : row + 128, :]
        q4 = jnp.concatenate([q4[:, h * 128 : (h + 1) * 128] for h in range(4)], axis=0)
        return nt_dot(q4, kv_ref[k0 : k0 + width[i], 0:128])

    def finish(n, m, i, s):
        row, k0 = m * 512 + i * 128, m * 512 + first[i]
        bias = bias_ref[m, i, :, 0 : width[i]]
        s = (s.reshape(4, 128, width[i]) + bias[None]).reshape(512, width[i])
        top = jnp.max(s, axis=1, keepdims=True) * RATE
        p = jnp.exp2(s * RATE - top).astype(BF16)
        total = jnp.sum(p.astype(F32), axis=1, keepdims=True)
        o = dot(p, kv_ref[k0 : k0 + width[i], 128:256])
        o = (o * (1.0 / total)).astype(BF16)
        for h in range(4):
            ov[n, row : row + 128, h * 128 : (h + 1) * 128] = o[h * 128 : (h + 1) * 128]

    own_load.wait()

    def chunk(n, carry):
        load(n).wait()
        ahead = score(n, *steps[0])
        for at, step in enumerate(steps):
            s = ahead
            if at + 1 < len(steps):
                ahead = score(n, *steps[at + 1])
            finish(n, *step, s)
        store(n).start()
        return carry

    lax.fori_loop(0, 4, chunk, 0)
    for n in range(4):
        store(n).wait()


def decode(
    plen, qx_hbm, own_hbm, kv_hbm, cache_ref, out_hbm, qx, own_ref, kv_ref, ov, of, kvi, ownkv, lens,
    wide, kv_sem, in_sem, out_sem,
):
    own_load = pltpu.make_async_copy(own_hbm, own_ref, kv_sem.at[0])
    own_load.start()
    kv_load = pltpu.make_async_copy(kv_hbm, kv_ref, kv_sem.at[1])
    kv_load.start()

    def bring(g):
        part = pl.ds(pl.multiple_of(g * 8, 8), 8)
        return pltpu.make_async_copy(qx_hbm.at[part], qx.at[part], in_sem.at[g])

    for g in range(8):
        bring(g).start()

    def store(m, b, j):
        at = pl.multiple_of(j * 512 + m * 256 + b * 32, 32)
        here = ov.at[m, j, pl.ds(pl.multiple_of(b * 32, 32), 32)]
        return pltpu.make_async_copy(here, out_hbm.at[pl.ds(at, 32)], out_sem.at[m * 16 + b * 2 + j])

    def narrow(m, b):
        for j in range(2):
            for h in range(16):
                ov[m, j, pl.ds(pl.multiple_of(b * 32, 32), 32), h * 128 : (h + 1) * 128] = of[
                    m, j * 8 + b, h
                ].astype(BF16)

    def send(m, b):
        for j in range(2):
            store(m, b, j).start()

    kvi[2048:2560, :] = jnp.zeros((512, 128), F32)
    same = ((iota((256, 256), 0) >> 2) & 7) == (iota((256, 256), 1) & 7)
    same = same.astype(F32).astype(BF16)
    spot, block = iota((64, 256), 1), iota((64, 256), 0)
    mine = ((spot >> 5) == (block & 7)) & ((spot & 3) == ((block >> 3) & 3))
    reach = cache_ref[:, :].astype(F32)
    reach = jnp.where(block < 32, reach[:, 0:256], reach[:, 256:512])
    lens[...] = dot(jnp.where(mine, reach, 0.0).astype(BF16), same).reshape(8, 8, 256)
    own_load.wait()

    def own_part(n, carry):
        m, b = n >> 3, n & 7
        for x in range(2):

            def part(j):
                at = pl.multiple_of(j * 512 + m * 256 + b * 32, 32)
                return own_ref[pl.ds(at, 32), x * 128 : (x + 1) * 128]

            def to(c, rows):
                ownkv[x * 8 + m * 4 + c, pl.ds(pl.multiple_of(b * 16, 16), 16), :] = rows

            spread(wide.at[x], part, to)
        return carry

    lax.fori_loop(0, 16, own_part, 0, unroll=2)
    eye = (iota((128, 128), 0) == iota((128, 128), 1)).astype(F32).astype(BF16)
    for m in range(2):
        flat = nt_dot(eye, ownkv[8 + m * 4 : 12 + m * 4].reshape(512, 128)).astype(BF16)
        for c in range(4):
            ownkv[8 + m * 4 + c] = flat[:, c * 128 : (c + 1) * 128]
    kv_load.wait()
    kvi[pl.ds(0, 1024, stride=2), :] = kv_ref[:, 0:128].astype(F32)
    kvi[pl.ds(1, 1024, stride=2), :] = kv_ref[:, 128:256].astype(F32)
    lane, row = iota((16, 256), 1), iota((16, 256), 0)
    fits = ((row & 7) == (lane & 7)) & ((row >> 3) <= ((lane >> 3) & 1))
    own_bias = jnp.where(fits, 0.0, NEVER).astype(F32)
    band = iota((128, 256), 0) >> 4

    def group(tiles, m, c, begin):
        g = m * 4 + c
        size = tiles * 128
        at = 2 * (m * 512 + begin)
        keys = kvi[pl.ds(at, size, stride=2), :].astype(BF16)
        values = kvi[pl.ds(at + 1, size, stride=2), :].T.astype(BF16)
        values = jnp.concatenate([values, ownkv[8 + g]], axis=1)
        position = iota((size, 256), 0).astype(F32)

        def score(b):
            return nt_dot(jnp.concatenate([keys, ownkv[g, b * 16 : (b + 1) * 16]], axis=0), qx[g * 8 + b])

        def finish(b, s):
            inside = position < lens[g, b : b + 1, :]
            old = jnp.where(inside, s[:size], NEVER)
            new = s[size:] + own_bias
            top = jnp.maximum(
                jnp.max(old, axis=0, keepdims=True), jnp.max(new, axis=0, keepdims=True)
            )
            top = top * RATE
            old = jnp.exp2(old * RATE - top)
            new = jnp.exp2(new * RATE - top)
            total = jnp.sum(old, axis=0, keepdims=True) + jnp.sum(new, axis=0, keepdims=True)
            new = jnp.where(band == b, jnp.concatenate([new] * 8, axis=0), 0.0)
            p = jnp.concatenate([old.astype(BF16), new.astype(BF16)], axis=0)
            o = (dot(values, p) * (1.0 / total)).T
            for h in range(16):
                for j in range(2):
                    part = o[(h * 2 + j) * 8 : (h * 2 + j + 1) * 8]
                    of[m, j * 8 + b, h, pl.ds(c, 8, stride=4), :] = part

        scores = [score(b) for b in range(8)]
        for b in range(8):
            finish(b, scores[b])
        for b in range(2):
            narrow(1 - m, c * 2 + b)

    def one(g, begin):
        m, c = g >> 2, g & 3
        length = plen[m, c]
        begin = jnp.where(c == 0, 0, begin)
        bring(g).wait()
        pl.when(length <= 128)(lambda: group(1, m, c, begin))
        pl.when(length > 128)(lambda: group(2, m, c, begin))

        @pl.when(m == 1)
        def _():
            send(0, c * 2)
            send(0, c * 2 + 1)

        return begin + length

    lax.fori_loop(0, 8, one, jnp.int32(0))

    def tail(b, carry):
        narrow(1, b)
        send(1, b)
        return carry

    lax.fori_loop(0, 8, tail, 0)
    for m in range(2):
        for b in range(8):
            for j in range(2):
                store(m, b, j).wait()


def kernel(plen, q_hbm, qx_hbm, own_hbm, kv_hbm, cache_ref, out_hbm, *scratch):
    pq, qx, own_ref, kv_ref, po, bias, do, of, kvi, ownkv, lens, wide, kv_sem, in_sem, out_sem = scratch

    @pl.when(lax.axis_index("pool") != 0)
    def _():
        decode(
            plen, qx_hbm, own_hbm, kv_hbm, cache_ref, out_hbm, qx, own_ref, kv_ref, do, of, kvi,
            ownkv, lens, wide, kv_sem, in_sem, out_sem,
        )

    @pl.when(lax.axis_index("pool") == 0)
    def _():
        prefill(plen, q_hbm, own_hbm, out_hbm, pq, own_ref, po, bias, kv_sem, in_sem, out_sem)


def attend(plen, q, qx, own, kv, cache):
    vmem = pl.BlockSpec(memory_space=pltpu.VMEM)
    smem = pl.BlockSpec(memory_space=pltpu.SMEM)
    hbm = pl.BlockSpec(memory_space=pltpu.HBM)
    return pl.pallas_call(
        kernel,
        out_shape=jax.ShapeDtypeStruct((1024, 2048), BF16),
        in_specs=[smem, hbm, hbm, hbm, hbm, vmem],
        out_specs=hbm,
        scratch_shapes=[
            pltpu.VMEM((4, 1024, 512), BF16),
            pltpu.VMEM((64, 256, 128), BF16),
            pltpu.VMEM((1024, 256), BF16),
            pltpu.VMEM((1024, 256), BF16),
            pltpu.VMEM((4, 1024, 512), BF16),
            pltpu.VMEM((2, 4, 128, 384), F32),
            pltpu.VMEM((2, 2, 256, 2048), BF16),
            pltpu.VMEM((2, 16, 16, 32, 128), F32),
            pltpu.VMEM((2560, 128), F32),
            pltpu.VMEM((16, 128, 128), BF16),
            pltpu.VMEM((8, 8, 256), F32),
            pltpu.VMEM((2, 2, 32, 128), F32),
            pltpu.SemaphoreType.DMA((2,)),
            pltpu.SemaphoreType.DMA((8,)),
            pltpu.SemaphoreType.DMA((32,)),
        ],
        compiler_params=pltpu.CompilerParams(vmem_limit_bytes=40 * 1024 * 1024),
    )(plen, q, qx, own, kv, cache)


def body(queries, keys_values, prompt_lengths, cache_lengths, section_map):
    section = lax.axis_index("section")
    pool = lax.axis_index("pool")
    count = lax.axis_size("section")
    layers = jnp.arange(count, dtype=jnp.int32)
    ahead = jnp.where(layers == section, (section_map - section + count) % count, 0)
    behind = jnp.where(section_map == section, (section - layers + count) % count, 0)
    apart = jnp.sum(jnp.where(pool == 0, ahead, behind))
    q = queries[0, 0]
    kv = keys_values[0, 0]
    cache = cache_lengths[None, :]

    def route(by):
        pairs = [(2 * s, 2 * ((s + by) % count) + 1) for s in range(count)]

        return lambda kv, q: (lax.ppermute(kv, ("section", "pool"), pairs), regroup(q))

    arrived, qx = lax.switch(apart, [route(by) for by in range(count)], kv, q)
    out = attend(prompt_lengths, q, qx, kv, arrived, cache)
    return out[None, None]


def solution(mesh):
    return jax.shard_map(
        body,
        mesh=mesh,
        in_specs=(
            P("pool", "section", None, "tensor"),
            P("pool", "section", None, "tensor"),
            P(),
            P(),
            P(),
        ),
        out_specs=P("pool", "section", None, "tensor"),
        check_vma=False,
    )
```

```python
import functools
import math

import jax
import jax.numpy as jnp
from jax import lax
from jax.experimental import pallas as pl
from jax.experimental.pallas import tpu as pltpu
from jax.sharding import PartitionSpec as P

HEAD_SIZE = 128
RATE = HEAD_SIZE ** (-0.5) * math.log2(math.e)
NEVER = -1e30
F32 = jnp.float32
BF16 = jnp.bfloat16


def nt_dot(a, b):
    return lax.dot_general(a, b, (((1,), (1,)), ((), ())), preferred_element_type=F32)


def dot(a, b):
    return jnp.dot(a, b, preferred_element_type=F32)


def iota(shape, dim):
    return lax.broadcasted_iota(jnp.int32, shape, dim)


def spread(wide, part, to):
    for j in range(2):
        wide[j] = part(j).astype(F32)
    for c in range(4):
        pair = [wide[j, pl.ds(c, 8, stride=4), :] for j in range(2)]
        to(c, jnp.concatenate(pair, axis=0).astype(BF16))


def regroup_kernel(q_hbm, qx, qv, wide, in_sem):
    @pl.when(lax.axis_index("pool") != 0)
    def _():
        def load(n):
            part = pl.ds(pl.multiple_of(n * 256, 256), 256)
            return pltpu.make_async_copy(q_hbm.at[part], qv.at[n], in_sem.at[n])

        lax.fori_loop(0, 4, lambda n, carry: (load(n).start(), carry)[1], 0)
        lax.fori_loop(0, 4, lambda n, carry: (load(n).wait(), carry)[1], 0)

        def piece(n, carry):
            m, b, h = n >> 7, (n >> 4) & 7, n & 15

            def part(j):
                lanes = pl.ds(pl.multiple_of(h * 128, 128), 128)
                return qv[j * 2 + m, pl.ds(pl.multiple_of(b * 32, 32), 32), lanes]

            def to(c, block):
                qx[(m * 4 + c) * 8 + b, pl.ds(pl.multiple_of(h * 16, 16), 16), :] = block

            spread(wide, part, to)
            return carry

        lax.fori_loop(0, 256, piece, 0)


def regroup(q):
    hbm = pl.BlockSpec(memory_space=pltpu.HBM)
    return pl.pallas_call(
        regroup_kernel,
        out_shape=jax.ShapeDtypeStruct((64, 256, 128), BF16),
        in_specs=[hbm],
        out_specs=pl.BlockSpec(memory_space=pltpu.VMEM),
        scratch_shapes=[
            pltpu.VMEM((4, 256, 2048), BF16),
            pltpu.VMEM((2, 32, 128), F32),
            pltpu.SemaphoreType.DMA((4,)),
        ],
        compiler_params=pltpu.CompilerParams(vmem_limit_bytes=14 * 1024 * 1024),
    )(q)


def prefill(plen, q_hbm, own_hbm, out_hbm, qv, kv_ref, ov, bias_ref, kv_sem, in_sem, out_sem):
    def columns(n):
        return pl.ds(pl.multiple_of(n * 512, 512), 512)

    def load(n):
        return pltpu.make_async_copy(q_hbm.at[:, columns(n)], qv.at[n], in_sem.at[n])

    def store(n):
        return pltpu.make_async_copy(ov.at[n], out_hbm.at[:, columns(n)], out_sem.at[n])

    own_load = pltpu.make_async_copy(own_hbm, kv_ref, kv_sem.at[0])
    own_load.start()
    for n in range(4):
        load(n).start()
    steps = [(m, i) for m in range(2) for i in range(4)]
    first = [max(0, i - 2) * 128 for i in range(4)]
    width = [(i + 1) * 128 - first[i] for i in range(4)]
    for m, i in steps:
        token = iota((128, width[i]), 0) + i * 128
        key = iota((128, width[i]), 1) + first[i]
        begin = jnp.zeros((128, width[i]), jnp.int32)
        end = jnp.int32(0)
        for c in range(4):
            end = end + plen[m, c]
            begin = jnp.where(token >= end, end, begin)
        allowed = (key >= begin) & (key <= token)
        bias_ref[m, i, :, 0 : width[i]] = jnp.where(allowed, 0.0, NEVER).astype(F32)

    def score(n, m, i):
        row, k0 = m * 512 + i * 128, m * 512 + first[i]
        q4 = qv[n, row : row + 128, :]
        q4 = jnp.concatenate([q4[:, h * 128 : (h + 1) * 128] for h in range(4)], axis=0)
        return nt_dot(q4, kv_ref[k0 : k0 + width[i], 0:128])

    def finish(n, m, i, s):
        row, k0 = m * 512 + i * 128, m * 512 + first[i]
        bias = bias_ref[m, i, :, 0 : width[i]]
        s = (s.reshape(4, 128, width[i]) + bias[None]).reshape(512, width[i])
        top = jnp.max(s, axis=1, keepdims=True) * RATE
        p = jnp.exp2(s * RATE - top).astype(BF16)
        total = jnp.sum(p.astype(F32), axis=1, keepdims=True)
        o = dot(p, kv_ref[k0 : k0 + width[i], 128:256])
        o = (o * (1.0 / total)).astype(BF16)
        for h in range(4):
            ov[n, row : row + 128, h * 128 : (h + 1) * 128] = o[h * 128 : (h + 1) * 128]

    own_load.wait()

    def chunk(n, carry):
        load(n).wait()
        ahead = score(n, *steps[0])
        for at, step in enumerate(steps):
            s = ahead
            if at + 1 < len(steps):
                ahead = score(n, *steps[at + 1])
            finish(n, *step, s)
        store(n).start()
        return carry

    lax.fori_loop(0, 4, chunk, 0)
    for n in range(4):
        store(n).wait()


def decode(
    plen, qx_hbm, own_hbm, kv_hbm, cache_ref, out_hbm, qx, own_ref, kv_ref, ov, of, kvi, ownkv, lens,
    wide, kv_sem, in_sem, out_sem,
):
    own_load = pltpu.make_async_copy(own_hbm, own_ref, kv_sem.at[0])
    own_load.start()
    kv_load = pltpu.make_async_copy(kv_hbm, kv_ref, kv_sem.at[1])
    kv_load.start()

    def bring(g):
        part = pl.ds(pl.multiple_of(g * 8, 8), 8)
        return pltpu.make_async_copy(qx_hbm.at[part], qx.at[part], in_sem.at[g])

    for g in range(8):
        bring(g).start()

    def store(m, b, j):
        at = pl.multiple_of(j * 512 + m * 256 + b * 32, 32)
        here = ov.at[m, j, pl.ds(pl.multiple_of(b * 32, 32), 32)]
        return pltpu.make_async_copy(here, out_hbm.at[pl.ds(at, 32)], out_sem.at[m * 16 + b * 2 + j])

    def narrow(m, b):
        for j in range(2):
            for h in range(16):
                ov[m, j, pl.ds(pl.multiple_of(b * 32, 32), 32), h * 128 : (h + 1) * 128] = of[
                    m, j * 8 + b, h
                ].astype(BF16)

    def send(m, b):
        for j in range(2):
            store(m, b, j).start()

    kvi[2048:2560, :] = jnp.zeros((512, 128), F32)
    same = ((iota((256, 256), 0) >> 2) & 7) == (iota((256, 256), 1) & 7)
    same = same.astype(F32).astype(BF16)
    spot, block = iota((64, 256), 1), iota((64, 256), 0)
    mine = ((spot >> 5) == (block & 7)) & ((spot & 3) == ((block >> 3) & 3))
    reach = cache_ref[:, :].astype(F32)
    reach = jnp.where(block < 32, reach[:, 0:256], reach[:, 256:512])
    lens[...] = dot(jnp.where(mine, reach, 0.0).astype(BF16), same).reshape(8, 8, 256)
    own_load.wait()

    def own_part(n, carry):
        m, b = n >> 3, n & 7
        for x in range(2):

            def part(j):
                at = pl.multiple_of(j * 512 + m * 256 + b * 32, 32)
                return own_ref[pl.ds(at, 32), x * 128 : (x + 1) * 128]

            def to(c, rows):
                ownkv[x * 8 + m * 4 + c, pl.ds(pl.multiple_of(b * 16, 16), 16), :] = rows

            spread(wide.at[x], part, to)
        return carry

    lax.fori_loop(0, 16, own_part, 0, unroll=2)
    eye = (iota((128, 128), 0) == iota((128, 128), 1)).astype(F32).astype(BF16)
    for m in range(2):
        flat = nt_dot(eye, ownkv[8 + m * 4 : 12 + m * 4].reshape(512, 128)).astype(BF16)
        for c in range(4):
            ownkv[8 + m * 4 + c] = flat[:, c * 128 : (c + 1) * 128]
    kv_load.wait()
    kvi[pl.ds(0, 1024, stride=2), :] = kv_ref[:, 0:128].astype(F32)
    kvi[pl.ds(1, 1024, stride=2), :] = kv_ref[:, 128:256].astype(F32)
    lane, row = iota((16, 256), 1), iota((16, 256), 0)
    fits = ((row & 7) == (lane & 7)) & ((row >> 3) <= ((lane >> 3) & 1))
    own_bias = jnp.where(fits, 0.0, NEVER).astype(F32)

    def group(size, m, c, begin):
        g = m * 4 + c
        at = 2 * (m * 512 + begin)
        keys = kvi[pl.ds(at, size, stride=2), :].astype(BF16)
        values = kvi[pl.ds(at + 1, size, stride=2), :].T.astype(BF16)
        own = ownkv[8 + g]
        values = [jnp.concatenate([values, own[:, k * 64 : (k + 1) * 64]], axis=1) for k in range(2)]
        position = iota((size, 256), 0).astype(F32)

        def score(b):
            return nt_dot(jnp.concatenate([keys, ownkv[g, b * 16 : (b + 1) * 16]], axis=0), qx[g * 8 + b])

        def finish(b, s):
            inside = position < lens[g, b : b + 1, :]
            old = jnp.where(inside, s[:size], NEVER)
            new = s[size:] + own_bias
            top = jnp.maximum(
                jnp.max(old, axis=0, keepdims=True), jnp.max(new, axis=0, keepdims=True)
            )
            top = top * RATE
            old = jnp.exp2(old * RATE - top)
            new = jnp.exp2(new * RATE - top)
            total = jnp.sum(old, axis=0, keepdims=True) + jnp.sum(new, axis=0, keepdims=True)
            blank = jnp.zeros((16, 256), BF16)
            new = jnp.concatenate([new.astype(BF16) if k == (b & 3) else blank for k in range(4)], axis=0)
            p = jnp.concatenate([old.astype(BF16), new.astype(BF16)], axis=0)
            o = (dot(values[b >> 2], p) * (1.0 / total)).astype(BF16).T.astype(F32)
            for h in range(16):
                for j in range(2):
                    part = o[(h * 2 + j) * 8 : (h * 2 + j + 1) * 8]
                    of[m, j * 8 + b, h, pl.ds(c, 8, stride=4), :] = part

        scores = [score(b) for b in range(8)]
        for b in range(8):
            finish(b, scores[b])
        for b in range(2):
            narrow(1 - m, c * 2 + b)

    def one(g, begin):
        m, c = g >> 2, g & 3
        length = plen[m, c]
        begin = jnp.where(c == 0, 0, begin)
        bring(g).wait()
        for size in (64, 128, 192, 256):
            fits = (length > size - 64) & (length <= size)
            pl.when(fits)(functools.partial(group, size, m, c, begin))

        @pl.when(m == 1)
        def _():
            send(0, c * 2)
            send(0, c * 2 + 1)

        return begin + length

    lax.fori_loop(0, 8, one, jnp.int32(0))

    def tail(b, carry):
        narrow(1, b)
        send(1, b)
        return carry

    lax.fori_loop(0, 8, tail, 0)
    for m in range(2):
        for b in range(8):
            for j in range(2):
                store(m, b, j).wait()


def kernel(plen, q_hbm, qx_hbm, own_hbm, kv_hbm, cache_ref, out_hbm, *scratch):
    pq, qx, own_ref, kv_ref, po, bias, do, of, kvi, ownkv, lens, wide, kv_sem, in_sem, out_sem = scratch

    @pl.when(lax.axis_index("pool") != 0)
    def _():
        decode(
            plen, qx_hbm, own_hbm, kv_hbm, cache_ref, out_hbm, qx, own_ref, kv_ref, do, of, kvi,
            ownkv, lens, wide, kv_sem, in_sem, out_sem,
        )

    @pl.when(lax.axis_index("pool") == 0)
    def _():
        prefill(plen, q_hbm, own_hbm, out_hbm, pq, own_ref, po, bias, kv_sem, in_sem, out_sem)


def attend(plen, q, qx, own, kv, cache):
    vmem = pl.BlockSpec(memory_space=pltpu.VMEM)
    smem = pl.BlockSpec(memory_space=pltpu.SMEM)
    hbm = pl.BlockSpec(memory_space=pltpu.HBM)
    return pl.pallas_call(
        kernel,
        out_shape=jax.ShapeDtypeStruct((1024, 2048), BF16),
        in_specs=[smem, hbm, hbm, hbm, hbm, vmem],
        out_specs=hbm,
        scratch_shapes=[
            pltpu.VMEM((4, 1024, 512), BF16),
            pltpu.VMEM((64, 256, 128), BF16),
            pltpu.VMEM((1024, 256), BF16),
            pltpu.VMEM((1024, 256), BF16),
            pltpu.VMEM((4, 1024, 512), BF16),
            pltpu.VMEM((2, 4, 128, 384), F32),
            pltpu.VMEM((2, 2, 256, 2048), BF16),
            pltpu.VMEM((2, 16, 16, 32, 128), F32),
            pltpu.VMEM((2560, 128), F32),
            pltpu.VMEM((16, 128, 128), BF16),
            pltpu.VMEM((8, 8, 256), F32),
            pltpu.VMEM((2, 2, 32, 128), F32),
            pltpu.SemaphoreType.DMA((2,)),
            pltpu.SemaphoreType.DMA((8,)),
            pltpu.SemaphoreType.DMA((32,)),
        ],
        compiler_params=pltpu.CompilerParams(vmem_limit_bytes=40 * 1024 * 1024),
    )(plen, q, qx, own, kv, cache)


def body(queries, keys_values, prompt_lengths, cache_lengths, section_map):
    section = lax.axis_index("section")
    pool = lax.axis_index("pool")
    count = lax.axis_size("section")
    layers = jnp.arange(count, dtype=jnp.int32)
    ahead = jnp.where(layers == section, (section_map - section + count) % count, 0)
    behind = jnp.where(section_map == section, (section - layers + count) % count, 0)
    apart = jnp.sum(jnp.where(pool == 0, ahead, behind))
    q = queries[0, 0]
    kv = keys_values[0, 0]
    cache = cache_lengths[None, :]

    def route(by):
        pairs = [(2 * s, 2 * ((s + by) % count) + 1) for s in range(count)]

        return lambda kv, q: (lax.ppermute(kv, ("section", "pool"), pairs), regroup(q))

    arrived, qx = lax.switch(apart, [route(by) for by in range(count)], kv, q)
    out = attend(prompt_lengths, q, qx, kv, arrived, cache)
    return out[None, None]


def solution(mesh):
    return jax.shard_map(
        body,
        mesh=mesh,
        in_specs=(
            P("pool", "section", None, "tensor"),
            P("pool", "section", None, "tensor"),
            P(),
            P(),
            P(),
        ),
        out_specs=P("pool", "section", None, "tensor"),
        check_vma=False,
    )
```

```python
import functools
import math

import jax
import jax.numpy as jnp
from jax import lax
from jax.experimental import pallas as pl
from jax.experimental.pallas import tpu as pltpu
from jax.sharding import PartitionSpec as P

HEAD_SIZE = 128
RATE = HEAD_SIZE ** (-0.5) * math.log2(math.e)
NEVER = -1e30
F32 = jnp.float32
BF16 = jnp.bfloat16


def nt_dot(a, b):
    return lax.dot_general(a, b, (((1,), (1,)), ((), ())), preferred_element_type=F32)


def tn_dot(a, b):
    return lax.dot_general(a, b, (((0,), (0,)), ((), ())), preferred_element_type=F32)


def dot(a, b):
    return jnp.dot(a, b, preferred_element_type=F32)


def iota(shape, dim):
    return lax.broadcasted_iota(jnp.int32, shape, dim)


def spread(wide, part, to):
    for j in range(2):
        wide[j] = part(j).astype(F32)
    for c in range(4):
        pair = [wide[j, pl.ds(c, 8, stride=4), :] for j in range(2)]
        to(c, jnp.concatenate(pair, axis=0).astype(BF16))


def regroup_kernel(q_hbm, qx, qv, wide, in_sem):
    @pl.when(lax.axis_index("pool") != 0)
    def _():
        def load(n):
            part = pl.ds(pl.multiple_of(n * 256, 256), 256)
            return pltpu.make_async_copy(q_hbm.at[part], qv.at[n], in_sem.at[n])

        lax.fori_loop(0, 4, lambda n, carry: (load(n).start(), carry)[1], 0)
        lax.fori_loop(0, 4, lambda n, carry: (load(n).wait(), carry)[1], 0)

        def piece(n, carry):
            m, b, h = n >> 7, (n >> 4) & 7, n & 15

            def part(j):
                lanes = pl.ds(pl.multiple_of(h * 128, 128), 128)
                return qv[j * 2 + m, pl.ds(pl.multiple_of(b * 32, 32), 32), lanes]

            def to(c, block):
                qx[(m * 4 + c) * 8 + b, pl.ds(pl.multiple_of(h * 16, 16), 16), :] = block

            spread(wide, part, to)
            return carry

        lax.fori_loop(0, 256, piece, 0)


def regroup(q):
    hbm = pl.BlockSpec(memory_space=pltpu.HBM)
    return pl.pallas_call(
        regroup_kernel,
        out_shape=jax.ShapeDtypeStruct((64, 256, 128), BF16),
        in_specs=[hbm],
        out_specs=pl.BlockSpec(memory_space=pltpu.VMEM),
        scratch_shapes=[
            pltpu.VMEM((4, 256, 2048), BF16),
            pltpu.VMEM((2, 32, 128), F32),
            pltpu.SemaphoreType.DMA((4,)),
        ],
        compiler_params=pltpu.CompilerParams(vmem_limit_bytes=14 * 1024 * 1024),
    )(q)


def prefill(plen, q_hbm, own_hbm, out_hbm, qv, kv_ref, ov, bias_ref, kv_sem, in_sem, out_sem):
    def columns(n):
        return pl.ds(pl.multiple_of(n * 512, 512), 512)

    def load(n):
        return pltpu.make_async_copy(q_hbm.at[:, columns(n)], qv.at[n], in_sem.at[n])

    def store(n):
        return pltpu.make_async_copy(ov.at[n], out_hbm.at[:, columns(n)], out_sem.at[n])

    own_load = pltpu.make_async_copy(own_hbm, kv_ref, kv_sem.at[0])
    own_load.start()
    for n in range(4):
        load(n).start()
    steps = [(m, i) for m in range(2) for i in range(4)]
    first = [max(0, i - 2) * 128 for i in range(4)]
    width = [(i + 1) * 128 - first[i] for i in range(4)]
    for m, i in steps:
        token = iota((128, width[i]), 0) + i * 128
        key = iota((128, width[i]), 1) + first[i]
        begin = jnp.zeros((128, width[i]), jnp.int32)
        end = jnp.int32(0)
        for c in range(4):
            end = end + plen[m, c]
            begin = jnp.where(token >= end, end, begin)
        allowed = (key >= begin) & (key <= token)
        bias_ref[m, i, :, 0 : width[i]] = jnp.where(allowed, 0.0, NEVER).astype(F32)

    def score(n, m, i):
        row, k0 = m * 512 + i * 128, m * 512 + first[i]
        q4 = qv[n, row : row + 128, :]
        q4 = jnp.concatenate([q4[:, h * 128 : (h + 1) * 128] for h in range(4)], axis=0)
        return nt_dot(q4, kv_ref[k0 : k0 + width[i], 0:128])

    def finish(n, m, i, s):
        row, k0 = m * 512 + i * 128, m * 512 + first[i]
        bias = bias_ref[m, i, :, 0 : width[i]]
        s = (s.reshape(4, 128, width[i]) + bias[None]).reshape(512, width[i])
        top = jnp.max(s, axis=1, keepdims=True) * RATE
        p = jnp.exp2(s * RATE - top).astype(BF16)
        total = jnp.sum(p.astype(F32), axis=1, keepdims=True)
        o = dot(p, kv_ref[k0 : k0 + width[i], 128:256])
        o = (o * (1.0 / total)).astype(BF16)
        for h in range(4):
            ov[n, row : row + 128, h * 128 : (h + 1) * 128] = o[h * 128 : (h + 1) * 128]

    own_load.wait()

    def chunk(n, carry):
        load(n).wait()
        ahead = score(n, *steps[0])
        for at, step in enumerate(steps):
            s = ahead
            if at + 1 < len(steps):
                ahead = score(n, *steps[at + 1])
            finish(n, *step, s)
        store(n).start()
        return carry

    lax.fori_loop(0, 4, chunk, 0)
    for n in range(4):
        store(n).wait()


def decode(
    plen, qx_hbm, own_hbm, kv_hbm, cache_ref, out_hbm, qx, own_ref, kv_ref, ov, of, kvi, ownkv, lens,
    wide, kv_sem, in_sem, out_sem,
):
    own_load = pltpu.make_async_copy(own_hbm, own_ref, kv_sem.at[0])
    own_load.start()
    kv_load = pltpu.make_async_copy(kv_hbm, kv_ref, kv_sem.at[1])
    kv_load.start()

    def bring(g):
        part = pl.ds(pl.multiple_of(g * 8, 8), 8)
        return pltpu.make_async_copy(qx_hbm.at[part], qx.at[part], in_sem.at[g])

    for g in range(8):
        bring(g).start()

    def store(m, b, j):
        at = pl.multiple_of(j * 512 + m * 256 + b * 32, 32)
        here = ov.at[m, j, pl.ds(pl.multiple_of(b * 32, 32), 32)]
        return pltpu.make_async_copy(here, out_hbm.at[pl.ds(at, 32)], out_sem.at[m * 16 + b * 2 + j])

    def narrow(m, b):
        for j in range(2):
            for h in range(16):
                ov[m, j, pl.ds(pl.multiple_of(b * 32, 32), 32), h * 128 : (h + 1) * 128] = of[
                    m, j * 8 + b, h
                ].astype(BF16)

    def send(m, b):
        for j in range(2):
            store(m, b, j).start()

    kvi[2048:2560, :] = jnp.zeros((512, 128), F32)
    same = ((iota((256, 256), 0) >> 2) & 7) == (iota((256, 256), 1) & 7)
    same = same.astype(F32).astype(BF16)
    spot, block = iota((64, 256), 1), iota((64, 256), 0)
    mine = ((spot >> 5) == (block & 7)) & ((spot & 3) == ((block >> 3) & 3))
    reach = cache_ref[:, :].astype(F32)
    reach = jnp.where(block < 32, reach[:, 0:256], reach[:, 256:512])
    lens[...] = dot(jnp.where(mine, reach, 0.0).astype(BF16), same).reshape(8, 8, 256)
    own_load.wait()

    def own_part(n, carry):
        m, b = n >> 3, n & 7
        for x in range(2):

            def part(j):
                at = pl.multiple_of(j * 512 + m * 256 + b * 32, 32)
                return own_ref[pl.ds(at, 32), x * 128 : (x + 1) * 128]

            def to(c, rows):
                ownkv[x * 8 + m * 4 + c, pl.ds(pl.multiple_of(b * 16, 16), 16), :] = rows

            spread(wide.at[x], part, to)
        return carry

    lax.fori_loop(0, 16, own_part, 0, unroll=4)
    kv_load.wait()
    kvi[pl.ds(0, 1024, stride=2), :] = kv_ref[:, 0:128].astype(F32)
    kvi[pl.ds(1, 1024, stride=2), :] = kv_ref[:, 128:256].astype(F32)
    lane, row = iota((16, 256), 1), iota((16, 256), 0)
    fits = ((row & 7) == (lane & 7)) & ((row >> 3) <= ((lane >> 3) & 1))
    own_bias = jnp.where(fits, 0.0, NEVER).astype(F32)

    def group(size, m, c, begin):
        g = m * 4 + c
        at = 2 * (m * 512 + begin)
        keys = kvi[pl.ds(at, size, stride=2), :].astype(BF16)
        values = kvi[pl.ds(at + 1, size, stride=2), :].astype(BF16)
        own = ownkv[8 + g]
        position = iota((size, 256), 0).astype(F32)

        def score(b):
            return nt_dot(jnp.concatenate([keys, ownkv[g, b * 16 : (b + 1) * 16]], axis=0), qx[g * 8 + b])

        def weigh(b, s):
            inside = position < lens[g, b : b + 1, :]
            old = jnp.where(inside, s[:size], NEVER)
            new = s[size:] + own_bias
            top = jnp.maximum(
                jnp.max(old, axis=0, keepdims=True), jnp.max(new, axis=0, keepdims=True)
            )
            top = top * RATE
            old = jnp.exp2(old * RATE - top)
            new = jnp.exp2(new * RATE - top)
            total = jnp.sum(old, axis=0, keepdims=True) + jnp.sum(new, axis=0, keepdims=True)
            share = 1.0 / total
            new = (new * share).astype(BF16)
            blank = jnp.zeros((16, 256), BF16)
            new = [new if k == b % 2 else blank for k in range(2)]
            return jnp.concatenate([(old * share).astype(BF16), *new], axis=0)

        scores = [score(b) for b in range(8)]
        for first in range(0, 8, 2):
            p = [weigh(b, scores[b]) for b in range(first, first + 2)]
            v = jnp.concatenate([values, own[first * 16 : (first + 2) * 16]], axis=0)
            o = tn_dot(jnp.concatenate(p, axis=1), v)
            for k in range(2):
                for h in range(16):
                    for j in range(2):
                        part = (k * 32 + h * 2 + j) * 8
                        of[m, j * 8 + first + k, h, pl.ds(c, 8, stride=4), :] = o[part : part + 8]
        for b in range(2):
            narrow(1 - m, c * 2 + b)

    def one(g, begin):
        m, c = g >> 2, g & 3
        length = plen[m, c]
        begin = jnp.where(c == 0, 0, begin)
        bring(g).wait()
        for size in (64, 128, 192, 256):
            fits = (length > size - 64) & (length <= size)
            pl.when(fits)(functools.partial(group, size, m, c, begin))

        @pl.when(m == 1)
        def _():
            send(0, c * 2)
            send(0, c * 2 + 1)

        return begin + length

    lax.fori_loop(0, 8, one, jnp.int32(0))

    def tail(b, carry):
        narrow(1, b)
        send(1, b)
        return carry

    lax.fori_loop(0, 8, tail, 0)
    for m in range(2):
        for b in range(8):
            for j in range(2):
                store(m, b, j).wait()


def kernel(plen, q_hbm, qx_hbm, own_hbm, kv_hbm, cache_ref, out_hbm, *scratch):
    pq, qx, own_ref, kv_ref, po, bias, do, of, kvi, ownkv, lens, wide, kv_sem, in_sem, out_sem = scratch

    @pl.when(lax.axis_index("pool") != 0)
    def _():
        decode(
            plen, qx_hbm, own_hbm, kv_hbm, cache_ref, out_hbm, qx, own_ref, kv_ref, do, of, kvi,
            ownkv, lens, wide, kv_sem, in_sem, out_sem,
        )

    @pl.when(lax.axis_index("pool") == 0)
    def _():
        prefill(plen, q_hbm, own_hbm, out_hbm, pq, own_ref, po, bias, kv_sem, in_sem, out_sem)


def attend(plen, q, qx, own, kv, cache):
    vmem = pl.BlockSpec(memory_space=pltpu.VMEM)
    smem = pl.BlockSpec(memory_space=pltpu.SMEM)
    hbm = pl.BlockSpec(memory_space=pltpu.HBM)
    return pl.pallas_call(
        kernel,
        out_shape=jax.ShapeDtypeStruct((1024, 2048), BF16),
        in_specs=[smem, hbm, hbm, hbm, hbm, vmem],
        out_specs=hbm,
        scratch_shapes=[
            pltpu.VMEM((4, 1024, 512), BF16),
            pltpu.VMEM((64, 256, 128), BF16),
            pltpu.VMEM((1024, 256), BF16),
            pltpu.VMEM((1024, 256), BF16),
            pltpu.VMEM((4, 1024, 512), BF16),
            pltpu.VMEM((2, 4, 128, 384), F32),
            pltpu.VMEM((2, 2, 256, 2048), BF16),
            pltpu.VMEM((2, 16, 16, 32, 128), F32),
            pltpu.VMEM((2560, 128), F32),
            pltpu.VMEM((16, 128, 128), BF16),
            pltpu.VMEM((8, 8, 256), F32),
            pltpu.VMEM((2, 2, 32, 128), F32),
            pltpu.SemaphoreType.DMA((2,)),
            pltpu.SemaphoreType.DMA((8,)),
            pltpu.SemaphoreType.DMA((32,)),
        ],
        compiler_params=pltpu.CompilerParams(vmem_limit_bytes=40 * 1024 * 1024),
    )(plen, q, qx, own, kv, cache)


def body(queries, keys_values, prompt_lengths, cache_lengths, section_map):
    section = lax.axis_index("section")
    pool = lax.axis_index("pool")
    count = lax.axis_size("section")
    layers = jnp.arange(count, dtype=jnp.int32)
    ahead = jnp.where(layers == section, (section_map - section + count) % count, 0)
    behind = jnp.where(section_map == section, (section - layers + count) % count, 0)
    apart = jnp.sum(jnp.where(pool == 0, ahead, behind))
    q = queries[0, 0]
    kv = keys_values[0, 0]
    cache = cache_lengths[None, :]

    def route(by):
        pairs = [(2 * s, 2 * ((s + by) % count) + 1) for s in range(count)]

        return lambda kv, q: (lax.ppermute(kv, ("section", "pool"), pairs), regroup(q))

    arrived, qx = lax.switch(apart, [route(by) for by in range(count)], kv, q)
    out = attend(prompt_lengths, q, qx, kv, arrived, cache)
    return out[None, None]


def solution(mesh):
    return jax.shard_map(
        body,
        mesh=mesh,
        in_specs=(
            P("pool", "section", None, "tensor"),
            P("pool", "section", None, "tensor"),
            P(),
            P(),
            P(),
        ),
        out_specs=P("pool", "section", None, "tensor"),
        check_vma=False,
    )
```
